512 devices in a mesh: tm: 32 (over x, z), space: 16 (over y, core).
Axes of the slice: x: 4, y: 8, z: 8, core: 2. Of those that a mesh axis runs over, the one named last changes fastest.
Arguments:
- queries: bfloat16 [512, 32, 8, 2240], P('tm', 'space'), may hold values from -6 to 6
- keys: bfloat16 [512, 32, 8, 2240], P('tm', 'space'), may hold values from -12 to 12
- values: bfloat16 [512, 32, 8, 2240], P('tm', 'space'), may hold values from -6 to 6
- gain: float32 [2240], replicated, may hold values from 0.1 to 1.9
- conv_weight: float32 [9, 2240], replicated, may hold values from -2 to 2
Outputs:
- mixed: bfloat16 [512, 32, 8, 2240], P('tm', 'space')
The draws below stay inside these ranges and needn't reach their ends.
All inputs are finite; a program needn't handle non-finite values.
Results may differ from the reference program's by a relative error of at most 0.005.
Values may be sent and summed in bfloat16 or wider, within the bound.
No kernel may reach another device: no remote copies, remote signals or barrier semaphores. Data moves between devices by JAX's collectives and lax.ppermute only.
A program may use at most 128 MiB of HBM per device.

```python
import math
import jax
import jax.numpy as jnp
from jax import lax

HEAD_DIM = 112
D = 2240
FRAMES_BLK = 16
COLS = 8
GRID_ROWS = 32
FRAMES = 512


def draw_keys(key, part):
    key = jax.random.fold_in(key, 11)
    key_base, key_token = jax.random.split(key, 2)
    base = jax.random.normal(key_base, (FRAMES, GRID_ROWS, COLS, D), jnp.float32)
    blocks = FRAMES // FRAMES_BLK
    block_index = (jnp.arange(FRAMES) // FRAMES_BLK).astype(jnp.float32)
    rise = jnp.exp(math.log(3.0) * block_index / max(blocks - 1, 1))
    token_scale = jnp.exp(jax.random.uniform(key_token, (FRAMES, GRID_ROWS, COLS, 1), jnp.float32, math.log(0.3), math.log(3.0)))
    result = base * rise[:, None, None, None] * token_scale
    return jnp.clip(result, -12.0, 12.0).astype(jnp.bfloat16)


def block_scale(own_key, shape, cuts, least, largest):
    loudness, own = 1.0, jax.random.fold_in(own_key, 6)
    for position, shards_of in cuts:
        steps = jnp.exp(jax.random.uniform(jax.random.fold_in(own, position), (shards_of,), jnp.float32, least / len(cuts), largest / len(cuts)))
        loudness = loudness * jnp.repeat(steps, shape[position] // shards_of).reshape([-1 if axis == position else 1 for axis in range(len(shape))])
    return loudness


def noise(key, extent, scale, bound, shards=(), kind=jnp.bfloat16):
    array = scale * jax.random.normal(key, extent, jnp.float32)
    if shards:
        array = array * block_scale(key, extent, shards, -0.22, 0.18)
    return jnp.clip(array, -bound, bound).astype(kind)


def setup_inputs(seed: int = 0) -> dict:
    key_of = jax.random.split(jax.random.key(seed), 6)
    queries = noise(key_of[0], (FRAMES, GRID_ROWS, COLS, D), 1.0, 6.0, ((0, 32), (1, 16)))
    keys = draw_keys(jax.random.fold_in(key_of[5], 71), 0)
    values = noise(key_of[2], (FRAMES, GRID_ROWS, COLS, D), 1.0, 6.0, ((0, 32), (1, 16)))
    gain = jnp.clip(1.0 + 0.18 * jax.random.normal(key_of[3], (D,), jnp.float32), 0.1, 1.9)
    conv_weight = noise(key_of[4], (9, D), 0.33, 2.0, (), jnp.float32)
    return dict(queries=queries, keys=keys, values=values, gain=gain, conv_weight=conv_weight)


EPS = 1e-06

def reference(queries, keys, values, gain, conv_weight):
    blocks = FRAMES // FRAMES_BLK
    head_count = D // HEAD_DIM

    def block_state(index):
        start = (index * FRAMES_BLK).astype(jnp.int32)
        kpart = lax.dynamic_slice_in_dim(keys, start, FRAMES_BLK, 0)
        vpart = lax.dynamic_slice_in_dim(values, start, FRAMES_BLK, 0)
        kflat = jnp.maximum(kpart, 0).astype(jnp.float32).reshape(-1, head_count, HEAD_DIM)
        vflat = vpart.astype(jnp.float32).reshape(-1, head_count, HEAD_DIM)
        state = jnp.einsum('thi,thj->hij', kflat, vflat, precision=lax.Precision.HIGHEST)
        return (state, lax.optimization_barrier(jnp.sum(kflat, axis=0)))
    states, sums = lax.map(block_state, jnp.arange(blocks, dtype=jnp.int32))
    prefix_state = jnp.cumsum(states, axis=0)
    prefix_ksum = jnp.cumsum(sums, axis=0)

    def readout(index):
        start = (index * FRAMES_BLK).astype(jnp.int32)
        qpart = lax.dynamic_slice_in_dim(queries, start, FRAMES_BLK, 0)
        qflat = jnp.maximum(qpart, 0).astype(jnp.float32).reshape(-1, head_count, HEAD_DIM)
        numer = jnp.einsum('thi,hij->thj', qflat, prefix_state[index], precision=lax.Precision.HIGHEST)
        denom = jnp.einsum('thi,hi->th', qflat, prefix_ksum[index], precision=lax.Precision.HIGHEST) + EPS
        attn = (numer / denom[..., None]).reshape(FRAMES_BLK, GRID_ROWS, COLS, D)
        meansq = lax.optimization_barrier(jnp.mean(attn * attn, axis=-1, keepdims=True))
        normed = (attn * lax.rsqrt(meansq + 1e-06) * gain).astype(jnp.bfloat16)
        padded = jnp.pad(normed, ((0, 0), (1, 1), (1, 1), (0, 0)))
        total = jnp.zeros((FRAMES_BLK, GRID_ROWS, COLS, D), jnp.float32)
        for row_off in range(3):
            for col_off in range(3):
                window = padded[:, row_off:row_off + GRID_ROWS, col_off:col_off + COLS, :]
                total = total + window.astype(jnp.float32) * conv_weight[3 * row_off + col_off]
        return total.astype(jnp.bfloat16)
    result = lax.map(readout, jnp.arange(blocks, dtype=jnp.int32))
    return result.reshape(FRAMES, GRID_ROWS, COLS, D)
```

```python
import jax
import jax.numpy as jnp
from jax import lax
from jax.experimental import pallas as pl
from jax.experimental.pallas import tpu as pltpu
from jax.sharding import Mesh, PartitionSpec as P

HEAD = 112
WIDTH = 2240
HEADS = WIDTH // HEAD
LANES = 128
TILES = 18
HALF_TILES = TILES // 2
HALF_ROWS = 1024
EPS = 1e-06
F32, BF16 = jnp.float32, jnp.bfloat16
VMEM_LIMIT = 48 * 1024 * 1024


def tile_heads(tile):
    first = tile + tile // 7
    return first, HEAD * (first + 1) - LANES * tile


def lane_range(tile):
    return LANES * tile, min(LANES * (tile + 1), WIDTH)


def state_kernel(core_ref, k_ref, v_ref, mine_ref, other_ref, kt_ref):
    core = core_ref[0]
    for tile in range(TILES):
        low, high = lane_range(tile)
        kt_ref[low:high, :] = jnp.maximum(k_ref[:, low:high], 0).T
    lane = lax.broadcasted_iota(jnp.int32, (HEAD, LANES), 1)
    ones = jnp.ones((k_ref.shape[0], LANES), BF16)
    for tile in range(TILES):
        first, end = tile_heads(tile)
        low, high = lane_range(tile)
        v = v_ref[:, low:high]
        if tile < TILES - 1:
            pair = jnp.dot(kt_ref[HEAD * first : HEAD * (first + 2), :], v, preferred_element_type=F32)
            state = jnp.where(lane < end, pair[:HEAD], pair[HEAD:])
        else:
            v = jnp.concatenate([v, jnp.zeros((v.shape[0], LANES - v.shape[1]), BF16)], axis=1)
            state = jnp.dot(kt_ref[HEAD * first : WIDTH, :], v, preferred_element_type=F32)
            for head in range(HEADS):
                ksum = jnp.dot(
                    kt_ref[HEAD * head : HEAD * (head + 1), :], ones, preferred_element_type=F32
                )
                state = jnp.where(lane == end + head, ksum, state)
        half, place = divmod(tile, HALF_TILES)
        rows = slice(HEAD * place, HEAD * (place + 1))

        @pl.when(core == half)
        def _():
            mine_ref[rows, :] = state

        @pl.when(core != half)
        def _():
            other_ref[rows, :] = state.astype(BF16)

    rest = slice(HEAD * HALF_TILES, HALF_ROWS)
    mine_ref[rest, :] = jnp.zeros((HALF_ROWS - HEAD * HALF_TILES, LANES), F32)
    other_ref[rest, :] = jnp.zeros((HALF_ROWS - HEAD * HALF_TILES, LANES), BF16)


def readout_kernel(core_ref, q_ref, mine_ref, other_ref, gain_ref, top_ref, low_ref, state_ref, attn_ref):
    core = core_ref[0]
    tokens = q_ref.shape[0]
    state_ref[core] = mine_ref[...]
    state_ref[1 - core] = other_ref[...]
    lane = lax.broadcasted_iota(jnp.int32, (HEAD, LANES), 1)
    zero = jnp.zeros((HEAD, LANES), BF16)

    def tile_state(tile):
        half, place = divmod(tile, HALF_TILES)
        return state_ref[half, HEAD * place : HEAD * (place + 1), :]

    last = tile_state(TILES - 1)
    last_end = tile_heads(TILES - 1)[1]
    square = jnp.zeros((tokens, LANES), F32)
    for tile in range(TILES):
        first, end = tile_heads(tile)
        heads = [h for h in (first, first + 1) if h < HEADS]
        state = tile_state(tile)
        start = HEAD * first // LANES * LANES
        stop = min(start + 3 * LANES, WIDTH)
        parts = []
        offset = HEAD * first - start
        if offset:
            parts.append(jnp.zeros((offset, 2 * LANES), BF16))
        for position, head in enumerate(heads):
            inside = (lane < end) if position == 0 else (lane >= end)
            ksum = jnp.broadcast_to(last[:, last_end + head : last_end + head + 1], (HEAD, LANES))
            parts.append(
                jnp.concatenate([jnp.where(inside, state, zero), jnp.where(inside, ksum, zero)], axis=1)
            )
        remain = stop - start - offset - HEAD * len(heads)
        if remain:
            parts.append(jnp.zeros((remain, 2 * LANES), BF16))
        weights = jnp.concatenate(parts, axis=0)
        q = jnp.maximum(q_ref[:, start:stop], 0)
        both = jnp.dot(q, weights, preferred_element_type=F32)
        attn = both[:, :LANES] / (both[:, LANES:] + EPS)
        if tile == TILES - 1:
            keep = lax.broadcasted_iota(jnp.int32, (tokens, LANES), 1) < end
            attn = jnp.where(keep, attn, 0.0)
        attn_ref[:, LANES * tile : LANES * (tile + 1)] = attn
        square = square + attn * attn
    scale = lax.rsqrt(jnp.sum(square, axis=1, keepdims=True) * (1.0 / WIDTH) + 1e-06)
    scale = jnp.broadcast_to(scale, (tokens, LANES))
    for tile in range(TILES):
        low, high = lane_range(tile)
        wide = high - low
        normed = attn_ref[:, low:high] * scale[:, :wide] * gain_ref[:, low:high]
        normed = normed.astype(BF16).astype(F32).reshape(tokens // 16, 2, 8, wide)
        top_ref[:, low:high] = normed[:, 0].reshape(tokens // 2, wide).astype(BF16)
        low_ref[:, low:high] = normed[:, 1].reshape(tokens // 2, wide).astype(BF16)


def conv_kernel(before_ref, top_ref, low_ref, after_ref, weight_ref, out_ref):
    tokens = top_ref.shape[0]
    frames = tokens // 8
    for tile in range(TILES):
        low, high = lane_range(tile)
        wide = high - low
        col = lax.broadcasted_iota(jnp.int32, (8, wide), 0)
        weights = []
        for tap in range(9):
            w = jnp.broadcast_to(weight_ref[tap : tap + 1, low:high], (8, wide))
            if tap % 3 == 0:
                w = jnp.where(col == 0, 0.0, w)
            if tap % 3 == 2:
                w = jnp.where(col == 7, 0.0, w)
            weights.append(w[None])
        totals = [jnp.zeros((frames, 8, wide), F32)] * 2
        for place, ref in enumerate((before_ref, top_ref, low_ref, after_ref)):
            row = ref[:, low:high].astype(F32).reshape(frames, 8, wide)
            moved = (pltpu.roll(row, 1, 1), row, pltpu.roll(row, 7, 1))
            for out_row in range(2):
                row_off = place - out_row
                if 0 <= row_off <= 2:
                    for col_off in range(3):
                        totals[out_row] = totals[out_row] + moved[col_off] * weights[3 * row_off + col_off]
        both = jnp.concatenate([totals[0][:, None], totals[1][:, None]], axis=1)
        out_ref[:, low:high] = both.reshape(2 * tokens, wide).astype(BF16)


def call(kernel, outs, in_specs, scratch=()):
    return pl.pallas_call(
        kernel,
        out_shape=outs,
        in_specs=in_specs,
        out_specs=jax.tree.map(lambda _: pl.BlockSpec(memory_space=pltpu.VMEM), outs),
        scratch_shapes=scratch,
        compiler_params=pltpu.CompilerParams(vmem_limit_bytes=VMEM_LIMIT),
    )


VM = pl.BlockSpec(memory_space=pltpu.VMEM)
SM = pl.BlockSpec(memory_space=pltpu.SMEM)


def shards(queries, keys, values, gain, conv_weight):
    frames, rows, cols, width = queries.shape
    tokens = frames * rows * cols
    shape = jax.ShapeDtypeStruct
    core = lax.axis_index("core").reshape(1).astype(jnp.int32)
    swap = [(0, 1), (1, 0)]

    mine, other = call(
        state_kernel,
        [shape((HALF_ROWS, LANES), F32), shape((HALF_ROWS, LANES), BF16)],
        [SM, VM, VM],
        [pltpu.VMEM((WIDTH, tokens), BF16)],
    )(core, keys.reshape(tokens, width), values.reshape(tokens, width))

    xs, ys, zs = lax.axis_size("x"), lax.axis_size("y"), lax.axis_size("z")
    chunk = HALF_ROWS // (xs * ys)
    half = (mine + lax.ppermute(other, "core", swap).astype(F32)).astype(BF16)
    pieces = lax.all_to_all(half.reshape(xs * ys, chunk, LANES), ("x", "y"), 0, 0, tiled=True)
    totals = jnp.sum(pieces.reshape(xs, ys, chunk, LANES).astype(F32), axis=1).astype(BF16)

    spread = jnp.broadcast_to(totals[None], (zs, xs, chunk, LANES))
    blocks = lax.all_to_all(spread, "z", 0, 0, tiled=True)
    earlier = (jnp.arange(zs) <= lax.axis_index("z")).astype(F32)[:, None, None, None]
    prefix = []
    before = jnp.zeros((chunk, LANES), F32)
    upto = jnp.sum(blocks.astype(F32) * earlier, axis=0)
    whole = jnp.sum(blocks.astype(F32), axis=0)
    for x in range(xs):
        prefix.append((before + upto[x]).astype(BF16))
        before = before + whole[x]
    prefix = jnp.broadcast_to(jnp.stack(prefix)[:, None], (xs, ys, chunk, LANES))
    held = lax.all_to_all(prefix.reshape(xs * ys, chunk, LANES), ("x", "y"), 0, 0, tiled=True)
    held = held.reshape(HALF_ROWS, LANES)
    taken = lax.ppermute(held, "core", swap)

    top, low = call(
        readout_kernel,
        [shape((tokens // 2, width), BF16)] * 2,
        [SM, VM, VM, VM, VM],
        [pltpu.VMEM((2, HALF_ROWS, LANES), BF16), pltpu.VMEM((tokens, TILES * LANES), F32)],
    )(core, queries.reshape(tokens, width), held, taken, gain.reshape(1, width))

    size = ys * 2
    up = [(i, i + 1) for i in range(size - 1)]
    down = [(i + 1, i) for i in range(size - 1)]
    before = lax.ppermute(low, ("y", "core"), up)
    after = lax.ppermute(top, ("y", "core"), down)
    out = call(conv_kernel, shape((tokens, width), BF16), [VM] * 5)(before, top, low, after, conv_weight)
    return out.reshape(frames, rows, cols, width)


def solution(mesh):
    fine = Mesh(mesh.devices.reshape(4, 8, 8, 2), ("x", "z", "y", "core"))
    tokens = P(("x", "z"), ("y", "core"), None, None)
    return jax.shard_map(
        shards, mesh=fine, in_specs=(tokens, tokens, tokens, P(), P()), out_specs=tokens, check_vma=False
    )
```

```python
import jax
import jax.numpy as jnp
from jax import lax
from jax.experimental import pallas as pl
from jax.experimental.pallas import tpu as pltpu
from jax.sharding import Mesh, PartitionSpec as P

HEAD = 112
WIDTH = 2240
HEADS = WIDTH // HEAD
LANES = 128
TILES = 18
HALF_TILES = TILES // 2
PREFIX_FLOPS = 100_000_000
STATE_VMEM = 55_200_000
CHUNKS = 4
HALF_ROWS = 1024
EPS = 1e-06
F32, BF16 = jnp.float32, jnp.bfloat16
VMEM_LIMIT = 48 * 1024 * 1024


def tile_heads(tile):
    first = tile + tile // 7
    return first, HEAD * (first + 1) - LANES * tile


def lane_range(tile):
    return LANES * tile, min(LANES * (tile + 1), WIDTH)


def state_kernel(core_ref, k_ref, v_ref, mine_ref, other_ref, k_buf, v_buf, kt_ref, sems):
    core = core_ref[0]
    tokens = k_buf.shape[0]
    rows = tokens // CHUNKS
    copies = []
    for which, (ref, buf) in enumerate(((k_ref, k_buf), (v_ref, v_buf))):
        for chunk in range(CHUNKS):
            part = slice(rows * chunk, rows * (chunk + 1))
            copies.append(pltpu.make_async_copy(ref.at[part], buf.at[part], sems.at[which, chunk]))
    for copy in copies:
        copy.start()
    for copy in copies[:CHUNKS]:
        copy.wait()
    for tile in range(TILES):
        low, high = lane_range(tile)
        kt_ref[low:high, :] = jnp.maximum(k_buf[:, low:high], 0).T
    for copy in copies[CHUNKS:]:
        copy.wait()
    lane = lax.broadcasted_iota(jnp.int32, (HEAD, LANES), 1)
    ones = jnp.ones((tokens, LANES), BF16)
    for tile in range(TILES):
        first, end = tile_heads(tile)
        low, high = lane_range(tile)
        v = v_buf[:, low:high]
        if tile < TILES - 1:
            pair = jnp.dot(kt_ref[HEAD * first : HEAD * (first + 2), :], v, preferred_element_type=F32)
            state = jnp.where(lane < end, pair[:HEAD], pair[HEAD:])
        else:
            v = jnp.concatenate([v, jnp.zeros((tokens, LANES - v.shape[1]), BF16)], axis=1)
            state = jnp.dot(kt_ref[HEAD * first : WIDTH, :], v, preferred_element_type=F32)
            for head in range(HEADS):
                ksum = jnp.dot(
                    kt_ref[HEAD * head : HEAD * (head + 1), :], ones, preferred_element_type=F32
                )
                state = jnp.where(lane == end + head, ksum, state)
        half, place = divmod(tile, HALF_TILES)
        part = slice(HEAD * place, HEAD * (place + 1))

        @pl.when(core == half)
        def _():
            mine_ref[part, :] = state

        @pl.when(core != half)
        def _():
            other_ref[part, :] = state.astype(BF16)

    rest = slice(HEAD * HALF_TILES, HALF_ROWS)
    mine_ref[rest, :] = jnp.zeros((HALF_ROWS - HEAD * HALF_TILES, LANES), F32)
    other_ref[rest, :] = jnp.zeros((HALF_ROWS - HEAD * HALF_TILES, LANES), BF16)


def totals_kernel(pieces_ref, out_ref):
    zs, xs = out_ref.shape[:2]
    ys = pieces_ref.shape[0] // xs
    for x in range(xs):
        total = pieces_ref[ys * x].astype(F32)
        for y in range(1, ys):
            total = total + pieces_ref[ys * x + y].astype(F32)
        total = total.astype(BF16)
        for z in range(zs):
            out_ref[z, x] = total


def prefix_kernel(place_ref, blocks_ref, out_ref):
    zs, xs = blocks_ref.shape[:2]
    ys = out_ref.shape[0] // xs
    place = place_ref[0]
    before = jnp.zeros(blocks_ref.shape[2:], F32)
    for x in range(xs):
        upto, whole = before, before
        for z in range(zs):
            block = blocks_ref[z, x].astype(F32)
            upto = upto + jnp.where(z <= place, block, 0.0)
            whole = whole + block
        state = upto.astype(BF16)
        for y in range(ys):
            out_ref[ys * x + y] = state
        before = whole


def border_kernel(q_ref, top_ref, low_ref):
    tokens = q_ref.shape[0]
    for tile in range(TILES):
        low, high = lane_range(tile)
        wide = high - low
        q = jnp.maximum(q_ref[:, low:high], 0).astype(F32).reshape(tokens // 16, 2, 8, wide)
        top_ref[:, low:high] = q[:, 0].reshape(tokens // 2, wide).astype(BF16)
        low_ref[:, low:high] = q[:, 1].reshape(tokens // 2, wide).astype(BF16)
    rest = (tokens // 2, TILES * LANES - WIDTH)
    top_ref[:, WIDTH:] = jnp.zeros(rest, BF16)
    low_ref[:, WIDTH:] = jnp.zeros(rest, BF16)


def readout_kernel(
    core_ref, before_ref, q_ref, after_ref, mine_ref, other_ref, gain_ref, weight_ref, out_ref,
    state_ref, own_attn, before_attn, after_attn, own_scale, before_scale, after_scale, taps, out_buf, sems
):
    core = core_ref[0]
    tokens = q_ref.shape[0]
    state_ref[core] = mine_ref[...]
    state_ref[1 - core] = other_ref[...]
    lane = lax.broadcasted_iota(jnp.int32, (HEAD, LANES), 1)
    zero = jnp.zeros((HEAD, LANES), BF16)

    def tile_state(tile):
        half, place = divmod(tile, HALF_TILES)
        return state_ref[half, HEAD * place : HEAD * (place + 1), :]

    groups = (
        (q_ref, own_attn, own_scale),
        (before_ref, before_attn, before_scale),
        (after_ref, after_attn, after_scale),
    )
    last = tile_state(TILES - 1)
    last_end = tile_heads(TILES - 1)[1]
    squares = [jnp.zeros((group[0].shape[0], LANES), F32) for group in groups]
    for tile in range(TILES):
        first, end = tile_heads(tile)
        heads = [h for h in (first, first + 1) if h < HEADS]
        state = tile_state(tile)
        start = HEAD * first // LANES * LANES
        stop = min(start + 3 * LANES, WIDTH)
        parts = []
        offset = HEAD * first - start
        if offset:
            parts.append(jnp.zeros((offset, 2 * LANES), BF16))
        for position, head in enumerate(heads):
            inside = (lane < end) if position == 0 else (lane >= end)
            ksum = jnp.broadcast_to(last[:, last_end + head : last_end + head + 1], (HEAD, LANES))
            parts.append(
                jnp.concatenate([jnp.where(inside, state, zero), jnp.where(inside, ksum, zero)], axis=1)
            )
        remain = stop - start - offset - HEAD * len(heads)
        if remain:
            parts.append(jnp.zeros((remain, 2 * LANES), BF16))
        weights = jnp.concatenate(parts, axis=0)
        for place, (ref, attn_ref, _) in enumerate(groups):
            q = jnp.maximum(ref[:, start:stop], 0)
            both = jnp.dot(q, weights, preferred_element_type=F32)
            attn = both[:, :LANES] / (both[:, LANES:] + EPS)
            if tile == TILES - 1:
                keep = lax.broadcasted_iota(jnp.int32, attn.shape, 1) < end
                attn = jnp.where(keep, attn, 0.0)
            attn_ref[:, LANES * tile : LANES * (tile + 1)] = attn
            squares[place] = squares[place] + attn * attn
    for square, (_, _, scale_ref) in zip(squares, groups):
        mean = jnp.sum(square, axis=1, keepdims=True) * (1.0 / WIDTH)
        scale_ref[...] = jnp.broadcast_to(lax.rsqrt(mean + 1e-06), scale_ref.shape)

    for tile in range(TILES):
        low, high = lane_range(tile)
        col = lax.broadcasted_iota(jnp.int32, (8, high - low), 0)
        for tap in range(9):
            weight = jnp.broadcast_to(weight_ref[tap : tap + 1, low:high], (8, high - low))
            if tap % 3 == 0:
                weight = jnp.where(col == 0, 0.0, weight)
            if tap % 3 == 2:
                weight = jnp.where(col == 7, 0.0, weight)
            taps[tap, :, low:high] = weight

    rows = tokens // CHUNKS
    frames = rows // 16

    def one_chunk(chunk, carry):
        own = pl.ds(pl.multiple_of(chunk * rows, rows), rows)
        side = pl.ds(pl.multiple_of(chunk * (rows // 2), rows // 2), rows // 2)
        for tile in range(TILES):
            low, high = lane_range(tile)
            wide = high - low
            gain = gain_ref[:, low:high]

            def normed(attn_ref, scale_ref, part):
                value = attn_ref[part, low:high] * scale_ref[part, :wide] * gain
                return value.astype(BF16).astype(F32)

            own_rows = normed(own_attn, own_scale, own).reshape(frames, 2, 8, wide)
            four = (
                normed(before_attn, before_scale, side).reshape(frames, 8, wide),
                own_rows[:, 0],
                own_rows[:, 1],
                normed(after_attn, after_scale, side).reshape(frames, 8, wide),
            )
            totals = [None, None]
            for place, row in enumerate(four):
                moved = (pltpu.roll(row, 1, 1), row, pltpu.roll(row, 7, 1))
                for out_row in range(2):
                    row_off = place - out_row
                    if 0 <= row_off <= 2:
                        for col_off in range(3):
                            term = moved[col_off] * taps[3 * row_off + col_off, :, low:high][None]
                            totals[out_row] = term if totals[out_row] is None else totals[out_row] + term
            both = jnp.concatenate([totals[0][:, None], totals[1][:, None]], axis=1)
            out_buf[own, low:high] = both.reshape(rows, wide).astype(BF16)
        pltpu.make_async_copy(out_buf.at[own], out_ref.at[own], sems.at[chunk]).start()
        return carry

    lax.fori_loop(0, CHUNKS, one_chunk, 0)
    for chunk in range(CHUNKS):
        part = slice(rows * chunk, rows * (chunk + 1))
        pltpu.make_async_copy(out_buf.at[part], out_ref.at[part], sems.at[chunk]).wait()


def call(kernel, outs, in_specs, out_specs, scratch=(), flops=1_000_000_000, vmem=VMEM_LIMIT):
    return pl.pallas_call(
        kernel,
        out_shape=outs,
        in_specs=in_specs,
        out_specs=out_specs,
        scratch_shapes=scratch,
        compiler_params=pltpu.CompilerParams(vmem_limit_bytes=vmem),
        cost_estimate=pl.CostEstimate(flops=flops, bytes_accessed=5_000_000, transcendentals=0),
    )


VM = pl.BlockSpec(memory_space=pltpu.VMEM)
SM = pl.BlockSpec(memory_space=pltpu.SMEM)
HB = pl.BlockSpec(memory_space=pltpu.HBM)


def shards(queries, keys, values, gain, conv_weight):
    frames, rows, cols, width = queries.shape
    tokens = frames * rows * cols
    shape = jax.ShapeDtypeStruct
    core = lax.axis_index("core").reshape(1).astype(jnp.int32)
    swap = [(0, 1), (1, 0)]

    mine, other = call(
        state_kernel,
        [shape((HALF_ROWS, LANES), F32), shape((HALF_ROWS, LANES), BF16)],
        [SM, HB, HB],
        [VM, VM],
        [
            pltpu.VMEM((tokens, width), BF16),
            pltpu.VMEM((tokens, width), BF16),
            pltpu.VMEM((width, tokens), BF16),
            pltpu.SemaphoreType.DMA((2, CHUNKS)),
        ],
        vmem=STATE_VMEM,
    )(core, keys.reshape(tokens, width), values.reshape(tokens, width))

    xs, ys, zs = lax.axis_size("x"), lax.axis_size("y"), lax.axis_size("z")
    chunk = HALF_ROWS // (xs * ys)
    half = (mine + lax.ppermute(other, "core", swap).astype(F32)).astype(BF16)
    pieces = lax.all_to_all(half.reshape(xs * ys, chunk, LANES), ("x", "y"), 0, 0, tiled=True)
    totals = call(totals_kernel, shape((zs, xs, chunk, LANES), BF16), [VM], VM)(pieces)

    totals, q_late = lax.optimization_barrier((totals, queries.reshape(tokens, width)))
    border = shape((tokens // 2, TILES * LANES), BF16)
    top, low = call(border_kernel, [border] * 2, [VM], [VM] * 2, flops=20_000_000_000)(q_late)
    size = ys * 2
    up = [(i, i + 1) for i in range(size - 1)]
    down = [(i + 1, i) for i in range(size - 1)]
    q_before = lax.ppermute(low, ("y", "core"), up)
    q_after = lax.ppermute(top, ("y", "core"), down)

    blocks = lax.all_to_all(totals, "z", 0, 0, tiled=True)
    place = lax.axis_index("z").reshape(1).astype(jnp.int32)
    prefix = call(prefix_kernel, shape((xs * ys, chunk, LANES), BF16), [SM, VM], VM, flops=PREFIX_FLOPS)(place, blocks)
    held = lax.all_to_all(prefix, ("x", "y"), 0, 0, tiled=True)
    held, q_before, q_after = lax.optimization_barrier((held.reshape(HALF_ROWS, LANES), q_before, q_after))
    taken = lax.ppermute(held, "core", swap)

    padded = TILES * LANES
    out = call(
        readout_kernel,
        shape((tokens, width), BF16),
        [SM] + [VM] * 7,
        HB,
        [
            pltpu.VMEM((2, HALF_ROWS, LANES), BF16),
            pltpu.VMEM((tokens, padded), F32),
            pltpu.VMEM((tokens // 2, padded), F32),
            pltpu.VMEM((tokens // 2, padded), F32),
            pltpu.VMEM((tokens, LANES), F32),
            pltpu.VMEM((tokens // 2, LANES), F32),
            pltpu.VMEM((tokens // 2, LANES), F32),
            pltpu.VMEM((9, 8, padded), F32),
            pltpu.VMEM((tokens, width), BF16),
            pltpu.SemaphoreType.DMA((CHUNKS,)),
        ],
    )(
        core, q_before, queries.reshape(tokens, width), q_after, held, taken,
        gain.reshape(1, width), conv_weight,
    )
    return out.reshape(frames, rows, cols, width)


def solution(mesh):
    fine = Mesh(mesh.devices.reshape(4, 8, 8, 2), ("x", "z", "y", "core"))
    tokens = P(("x", "z"), ("y", "core"), None, None)
    return jax.shard_map(
        shards, mesh=fine, in_specs=(tokens, tokens, tokens, P(), P()), out_specs=tokens, check_vma=False
    )
```

```python
import jax
import jax.numpy as jnp
from jax import lax
from jax.experimental import pallas as pl
from jax.experimental.pallas import tpu as pltpu
from jax.sharding import Mesh, PartitionSpec as P

HEAD = 112
WIDTH = 2240
HEADS = WIDTH // HEAD
LANES = 128
TILES = 18
HALF_TILES = TILES // 2
PREFIX_FLOPS = 100_000_000
STATE_VMEM = 55_200_000
CHUNKS = 4
HALF_ROWS = 1024
EPS = 1e-06
F32, BF16 = jnp.float32, jnp.bfloat16
VMEM_LIMIT = 48 * 1024 * 1024


def tile_heads(tile):
    first = tile + tile // 7
    return first, HEAD * (first + 1) - LANES * tile


def lane_range(tile):
    return LANES * tile, min(LANES * (tile + 1), WIDTH)


def state_kernel(core_ref, k_ref, v_ref, mine_ref, other_ref, k_buf, v_buf, kt_ref, state_ref, sems):
    core = core_ref[0]
    tokens = k_buf.shape[0]
    rows = tokens // CHUNKS
    copies = []
    for which, (ref, buf) in enumerate(((k_ref, k_buf), (v_ref, v_buf))):
        for chunk in range(CHUNKS):
            part = slice(rows * chunk, rows * (chunk + 1))
            copies.append(pltpu.make_async_copy(ref.at[part], buf.at[part], sems.at[which, chunk]))
    for copy in copies:
        copy.start()
    for copy in copies[:CHUNKS]:
        copy.wait()
    for tile in range(TILES):
        low, high = lane_range(tile)
        kt_ref[low:high, :] = jnp.maximum(k_buf[:, low:high], 0).T
    for copy in copies[CHUNKS:]:
        copy.wait()
    lane = lax.broadcasted_iota(jnp.int32, (HEAD, LANES), 1)
    ones = jnp.ones((tokens, LANES), BF16)
    for tile in range(TILES):
        first, end = tile_heads(tile)
        low, high = lane_range(tile)
        v = v_buf[:, low:high]
        if tile < TILES - 1:
            pair = jnp.dot(kt_ref[HEAD * first : HEAD * (first + 2), :], v, preferred_element_type=F32)
            state = jnp.where(lane < end, pair[:HEAD], pair[HEAD:])
        else:
            v = jnp.concatenate([v, jnp.zeros((tokens, LANES - v.shape[1]), BF16)], axis=1)
            state = jnp.dot(kt_ref[HEAD * first : WIDTH, :], v, preferred_element_type=F32)
            for head in range(HEADS):
                ksum = jnp.dot(
                    kt_ref[HEAD * head : HEAD * (head + 1), :], ones, preferred_element_type=F32
                )
                state = jnp.where(lane == end + head, ksum, state)
        half, place = divmod(tile, HALF_TILES)
        state_ref[half, HEAD * place : HEAD * (place + 1), :] = state
    rest = HEAD * HALF_TILES
    mine_ref[:rest, :] = state_ref[core]
    other_ref[:rest, :] = state_ref[1 - core].astype(BF16)
    mine_ref[rest:, :] = jnp.zeros((HALF_ROWS - rest, LANES), F32)
    other_ref[rest:, :] = jnp.zeros((HALF_ROWS - rest, LANES), BF16)


def totals_kernel(pieces_ref, out_ref):
    zs, xs = out_ref.shape[:2]
    ys = pieces_ref.shape[0] // xs
    for x in range(xs):
        total = pieces_ref[ys * x].astype(F32)
        for y in range(1, ys):
            total = total + pieces_ref[ys * x + y].astype(F32)
        total = total.astype(BF16)
        for z in range(zs):
            out_ref[z, x] = total


def prefix_kernel(place_ref, blocks_ref, out_ref):
    zs, xs = blocks_ref.shape[:2]
    ys = out_ref.shape[0] // xs
    place = place_ref[0]
    before = jnp.zeros(blocks_ref.shape[2:], F32)
    for x in range(xs):
        upto, whole = before, before
        for z in range(zs):
            block = blocks_ref[z, x].astype(F32)
            upto = upto + jnp.where(z <= place, block, 0.0)
            whole = whole + block
        state = upto.astype(BF16)
        for y in range(ys):
            out_ref[ys * x + y] = state
        before = whole


def border_kernel(q_ref, top_ref, low_ref):
    tokens = q_ref.shape[0]
    for tile in range(TILES):
        low, high = lane_range(tile)
        wide = high - low
        q = jnp.maximum(q_ref[:, low:high], 0).astype(F32).reshape(tokens // 16, 2, 8, wide)
        top_ref[:, low:high] = q[:, 0].reshape(tokens // 2, wide).astype(BF16)
        low_ref[:, low:high] = q[:, 1].reshape(tokens // 2, wide).astype(BF16)
    rest = (tokens // 2, TILES * LANES - WIDTH)
    top_ref[:, WIDTH:] = jnp.zeros(rest, BF16)
    low_ref[:, WIDTH:] = jnp.zeros(rest, BF16)


def heads_kernel(q_ref, before_ref, after_ref, gain_ref, weight_ref, out_ref, rows_ref):
    taps = weight_ref.shape[0]
    rows_ref[:taps, :WIDTH] = weight_ref[...]
    rows_ref[taps : taps + 1, :WIDTH] = gain_ref[...]
    place = 0
    for ref in (q_ref, before_ref, after_ref):
        rows = ref.shape[0]
        fill = jnp.zeros((rows, LANES - HEAD), BF16)
        for head in range(HEADS):
            q = jnp.maximum(ref[:, HEAD * head : HEAD * (head + 1)], 0)
            out_ref[place : place + rows, LANES * head : LANES * (head + 1)] = jnp.concatenate([q, fill], axis=1)
        place += rows


def readout_kernel(
    core_ref, q_ref, mine_ref, other_ref, rows_ref, out_ref, state_ref, attn_ref, scale_ref, taps, out_buf, sems
):
    core = core_ref[0]
    tokens = q_ref.shape[0] // 2
    state_ref[core] = mine_ref[...]
    state_ref[1 - core] = other_ref[...]
    lane = lax.broadcasted_iota(jnp.int32, (HEAD, LANES), 1)
    zero = jnp.zeros((HEAD, LANES), BF16)

    def tile_state(tile):
        half, place = divmod(tile, HALF_TILES)
        return state_ref[half, HEAD * place : HEAD * (place + 1), :]

    last = tile_state(TILES - 1)
    last_end = tile_heads(TILES - 1)[1]
    square = jnp.zeros((2 * tokens, LANES), F32)
    fill = jnp.zeros((LANES - HEAD, 2 * LANES), BF16)
    for tile in range(TILES):
        first, end = tile_heads(tile)
        heads = [h for h in (first, first + 1) if h < HEADS]
        state = tile_state(tile)
        parts = []
        for position, head in enumerate(heads):
            inside = (lane < end) if position == 0 else (lane >= end)
            ksum = jnp.broadcast_to(last[:, last_end + head : last_end + head + 1], (HEAD, LANES))
            parts.append(
                jnp.concatenate([jnp.where(inside, state, zero), jnp.where(inside, ksum, zero)], axis=1)
            )
            parts.append(fill)
        weights = jnp.concatenate(parts, axis=0)
        q = q_ref[:, LANES * first : LANES * (first + len(heads))]
        both = jnp.dot(q, weights, preferred_element_type=F32)
        attn = both[:, :LANES] / (both[:, LANES:] + EPS)
        if tile == TILES - 1:
            keep = lax.broadcasted_iota(jnp.int32, attn.shape, 1) < end
            attn = jnp.where(keep, attn, 0.0)
        square = square + attn * attn
        low, high = lane_range(tile)
        attn_ref[:, low:high] = attn[:, : high - low] * rows_ref[9:10, low:high]
    mean = jnp.sum(square, axis=1, keepdims=True) * (1.0 / WIDTH)
    scale_ref[...] = jnp.broadcast_to(lax.rsqrt(mean + 1e-06), scale_ref.shape)

    for tile in range(TILES):
        low, high = lane_range(tile)
        col = lax.broadcasted_iota(jnp.int32, (8, high - low), 0)
        for tap in range(9):
            weight = jnp.broadcast_to(rows_ref[tap : tap + 1, low:high], (8, high - low))
            if tap % 3 == 0:
                weight = jnp.where(col == 7, 0.0, weight)
            if tap % 3 == 2:
                weight = jnp.where(col == 0, 0.0, weight)
            taps[tap, :, low:high] = weight

    rows = tokens // CHUNKS
    frames = rows // 16

    def one_chunk(chunk, carry):
        own = pl.ds(pl.multiple_of(chunk * rows, rows), rows)
        before = pl.ds(pl.multiple_of(tokens + chunk * (rows // 2), rows // 2), rows // 2)
        after = pl.ds(pl.multiple_of(tokens + tokens // 2 + chunk * (rows // 2), rows // 2), rows // 2)
        for tile in range(TILES):
            low, high = lane_range(tile)
            wide = high - low

            def normed(part):
                value = attn_ref[part, low:high] * scale_ref[part, :wide]
                return value.astype(BF16).astype(F32).reshape(-1, 8, wide)

            own_rows = normed(own).reshape(frames, 2, 8, wide)
            four = (normed(before), own_rows[:, 0], own_rows[:, 1], normed(after))
            totals = []
            for out_row in range(2):
                sums = []
                for col_off in range(3):
                    terms = [
                        four[out_row + row_off] * taps[3 * row_off + col_off, :, low:high][None]
                        for row_off in range(3)
                    ]
                    sums.append(terms[0] + terms[1] + terms[2])
                totals.append(pltpu.roll(sums[0], 1, 1) + sums[1] + pltpu.roll(sums[2], 7, 1))
            both = jnp.concatenate([totals[0][:, None], totals[1][:, None]], axis=1)
            out_buf[own, low:high] = both.reshape(rows, wide).astype(BF16)
        pltpu.make_async_copy(out_buf.at[own], out_ref.at[own], sems.at[chunk]).start()
        return carry

    lax.fori_loop(0, CHUNKS, one_chunk, 0)
    for chunk in range(CHUNKS):
        part = slice(rows * chunk, rows * (chunk + 1))
        pltpu.make_async_copy(out_buf.at[part], out_ref.at[part], sems.at[chunk]).wait()


def call(kernel, outs, in_specs, out_specs, scratch=(), flops=1_000_000_000, vmem=VMEM_LIMIT):
    return pl.pallas_call(
        kernel,
        out_shape=outs,
        in_specs=in_specs,
        out_specs=out_specs,
        scratch_shapes=scratch,
        compiler_params=pltpu.CompilerParams(vmem_limit_bytes=vmem),
        cost_estimate=pl.CostEstimate(flops=flops, bytes_accessed=5_000_000, transcendentals=0),
    )


VM = pl.BlockSpec(memory_space=pltpu.VMEM)
SM = pl.BlockSpec(memory_space=pltpu.SMEM)
HB = pl.BlockSpec(memory_space=pltpu.HBM)


def shards(queries, keys, values, gain, conv_weight):
    frames, rows, cols, width = queries.shape
    tokens = frames * rows * cols
    shape = jax.ShapeDtypeStruct
    core = lax.axis_index("core").reshape(1).astype(jnp.int32)
    swap = [(0, 1), (1, 0)]

    mine, other = call(
        state_kernel,
        [shape((HALF_ROWS, LANES), F32), shape((HALF_ROWS, LANES), BF16)],
        [SM, HB, HB],
        [VM, VM],
        [
            pltpu.VMEM((tokens, width), BF16),
            pltpu.VMEM((tokens, width), BF16),
            pltpu.VMEM((width, tokens), BF16),
            pltpu.VMEM((2, HEAD * HALF_TILES, LANES), F32),
            pltpu.SemaphoreType.DMA((2, CHUNKS)),
        ],
        vmem=STATE_VMEM,
    )(core, keys.reshape(tokens, width), values.reshape(tokens, width))

    xs, ys, zs = lax.axis_size("x"), lax.axis_size("y"), lax.axis_size("z")
    chunk = HALF_ROWS // (xs * ys)
    half = (mine + lax.ppermute(other, "core", swap).astype(F32)).astype(BF16)
    pieces = lax.all_to_all(half.reshape(xs * ys, chunk, LANES), ("x", "y"), 0, 0, tiled=True)
    totals = call(totals_kernel, shape((zs, xs, chunk, LANES), BF16), [VM], VM)(pieces)

    totals, q_late = lax.optimization_barrier((totals, queries.reshape(tokens, width)))
    border = shape((tokens // 2, TILES * LANES), BF16)
    top, low = call(border_kernel, [border] * 2, [VM], [VM] * 2, flops=20_000_000_000)(q_late)
    size = ys * 2
    up = [(i, i + 1) for i in range(size - 1)]
    down = [(i + 1, i) for i in range(size - 1)]
    q_before = lax.ppermute(low, ("y", "core"), up)
    q_after = lax.ppermute(top, ("y", "core"), down)

    blocks = lax.all_to_all(totals, "z", 0, 0, tiled=True)
    place = lax.axis_index("z").reshape(1).astype(jnp.int32)
    prefix = call(prefix_kernel, shape((xs * ys, chunk, LANES), BF16), [SM, VM], VM, flops=PREFIX_FLOPS)(place, blocks)
    held = lax.all_to_all(prefix, ("x", "y"), 0, 0, tiled=True)
    by_head, taps = call(
        heads_kernel,
        [shape((2 * tokens, HEADS * LANES), BF16), shape((16, TILES * LANES), F32)],
        [VM] * 5,
        [VM] * 2,
    )(q_late, q_before, q_after, gain.reshape(1, width), conv_weight)
    held, by_head, taps = lax.optimization_barrier((held.reshape(HALF_ROWS, LANES), by_head, taps))
    taken = lax.ppermute(held, "core", swap)

    padded = TILES * LANES
    out = call(
        readout_kernel,
        shape((tokens, width), BF16),
        [SM] + [VM] * 4,
        HB,
        [
            pltpu.VMEM((2, HALF_ROWS, LANES), BF16),
            pltpu.VMEM((2 * tokens, padded), F32),
            pltpu.VMEM((2 * tokens, LANES), F32),
            pltpu.VMEM((9, 8, padded), F32),
            pltpu.VMEM((tokens, width), BF16),
            pltpu.SemaphoreType.DMA((CHUNKS,)),
        ],
    )(core, by_head, held, taken, taps)
    return out.reshape(frames, rows, cols, width)


def solution(mesh):
    fine = Mesh(mesh.devices.reshape(4, 8, 8, 2), ("x", "z", "y", "core"))
    tokens = P(("x", "z"), ("y", "core"), None, None)
    return jax.shard_map(
        shards, mesh=fine, in_specs=(tokens, tokens, tokens, P(), P()), out_specs=tokens, check_vma=False
    )
```

```python
import jax
import jax.numpy as jnp
from jax import lax
from jax.experimental import pallas as pl
from jax.experimental.pallas import tpu as pltpu
from jax.sharding import Mesh, PartitionSpec as P

HEAD = 112
WIDTH = 2240
HEADS = WIDTH // HEAD
LANES = 128
TILES = 18
HALF_TILES = TILES // 2
PREFIX_FLOPS = 100_000_000
STATE_VMEM = 55_200_000
CHUNKS = 4
HALF_ROWS = 1024
EPS = 1e-06
F32, BF16 = jnp.float32, jnp.bfloat16
VMEM_LIMIT = 48 * 1024 * 1024


def tile_heads(tile):
    first = tile + tile // 7
    return first, HEAD * (first + 1) - LANES * tile


def lane_range(tile):
    return LANES * tile, min(LANES * (tile + 1), WIDTH)


def state_kernel(core_ref, k_ref, v_ref, mine_ref, other_ref, k_buf, v_buf, kt_ref, state_ref, sems):
    core = core_ref[0]
    tokens = k_buf.shape[0]
    rows = tokens // CHUNKS
    copies = []
    for which, (ref, buf) in enumerate(((k_ref, k_buf), (v_ref, v_buf))):
        for chunk in range(CHUNKS):
            part = slice(rows * chunk, rows * (chunk + 1))
            copies.append(pltpu.make_async_copy(ref.at[part], buf.at[part], sems.at[which, chunk]))
    for copy in copies:
        copy.start()
    for copy in copies[:CHUNKS]:
        copy.wait()
    for tile in range(TILES):
        low, high = lane_range(tile)
        kt_ref[low:high, :] = jnp.maximum(k_buf[:, low:high], 0).T
    for copy in copies[CHUNKS:]:
        copy.wait()
    lane = lax.broadcasted_iota(jnp.int32, (HEAD, LANES), 1)
    ones = jnp.ones((tokens, LANES), BF16)
    for tile in range(TILES):
        first, end = tile_heads(tile)
        low, high = lane_range(tile)
        v = v_buf[:, low:high]
        if tile < TILES - 1:
            pair = jnp.dot(kt_ref[HEAD * first : HEAD * (first + 2), :], v, preferred_element_type=F32)
            state = jnp.where(lane < end, pair[:HEAD], pair[HEAD:])
        else:
            v = jnp.concatenate([v, jnp.zeros((tokens, LANES - v.shape[1]), BF16)], axis=1)
            state = jnp.dot(kt_ref[HEAD * first : WIDTH, :], v, preferred_element_type=F32)
            for head in range(HEADS):
                ksum = jnp.dot(
                    kt_ref[HEAD * head : HEAD * (head + 1), :], ones, preferred_element_type=F32
                )
                state = jnp.where(lane == end + head, ksum, state)
        half, place = divmod(tile, HALF_TILES)
        state_ref[half, HEAD * place : HEAD * (place + 1), :] = state
    rest = HEAD * HALF_TILES
    mine_ref[:rest, :] = state_ref[core]
    other_ref[:rest, :] = state_ref[1 - core].astype(BF16)
    mine_ref[rest:, :] = jnp.zeros((HALF_ROWS - rest, LANES), F32)
    other_ref[rest:, :] = jnp.zeros((HALF_ROWS - rest, LANES), BF16)


def totals_kernel(pieces_ref, out_ref):
    zs = out_ref.shape[0]
    pieces, chunk = pieces_ref.shape[:2]
    xs = out_ref.shape[1] // chunk
    ys = pieces // xs
    for x in range(xs):
        total = pieces_ref[ys * x].astype(F32)
        for y in range(1, ys):
            total = total + pieces_ref[ys * x + y].astype(F32)
        total = total.astype(BF16)
        for z in range(zs):
            out_ref[z, chunk * x : chunk * (x + 1), :] = total


def prefix_kernel(place_ref, blocks_ref, out_ref):
    zs = blocks_ref.shape[0]
    pieces, chunk = out_ref.shape[:2]
    xs = blocks_ref.shape[1] // chunk
    ys = pieces // xs
    place = place_ref[0]
    before = jnp.zeros((chunk, LANES), F32)
    for x in range(xs):
        upto, whole = before, before
        for z in range(zs):
            block = blocks_ref[z, chunk * x : chunk * (x + 1), :].astype(F32)
            upto = upto + jnp.where(z <= place, block, 0.0)
            whole = whole + block
        state = upto.astype(BF16)
        for y in range(ys):
            out_ref[ys * x + y] = state
        before = whole


def border_kernel(q_ref, top_ref, low_ref):
    tokens = q_ref.shape[0]
    for tile in range(TILES):
        low, high = lane_range(tile)
        wide = high - low
        q = jnp.maximum(q_ref[:, low:high], 0).astype(F32).reshape(tokens // 16, 2, 8, wide)
        top_ref[:, low:high] = q[:, 0].reshape(tokens // 2, wide).astype(BF16)
        low_ref[:, low:high] = q[:, 1].reshape(tokens // 2, wide).astype(BF16)
    rest = (tokens // 2, TILES * LANES - WIDTH)
    top_ref[:, WIDTH:] = jnp.zeros(rest, BF16)
    low_ref[:, WIDTH:] = jnp.zeros(rest, BF16)


def heads_kernel(q_ref, before_ref, after_ref, gain_ref, weight_ref, out_ref, rows_ref):
    taps = weight_ref.shape[0]
    rows_ref[:taps, :WIDTH] = weight_ref[...]
    rows_ref[taps : taps + 1, :WIDTH] = gain_ref[...]
    place = 0
    for ref in (q_ref, before_ref, after_ref):
        rows = ref.shape[0]
        fill = jnp.zeros((rows, LANES - HEAD), BF16)
        for head in range(HEADS):
            q = jnp.maximum(ref[:, HEAD * head : HEAD * (head + 1)], 0)
            out_ref[place : place + rows, LANES * head : LANES * (head + 1)] = jnp.concatenate([q, fill], axis=1)
        place += rows


def readout_kernel(
    q_ref, state_ref, rows_ref, out_ref, attn_ref, scale_ref, taps, out_buf, sems
):
    tokens = q_ref.shape[0] // 2
    lane = lax.broadcasted_iota(jnp.int32, (HEAD, LANES), 1)
    zero = jnp.zeros((HEAD, LANES), BF16)

    def tile_state(tile):
        half, place = divmod(tile, HALF_TILES)
        return state_ref[half, HEAD * place : HEAD * (place + 1), :]

    last = tile_state(TILES - 1)
    last_end = tile_heads(TILES - 1)[1]
    square = jnp.zeros((2 * tokens, LANES), F32)
    fill = jnp.zeros((LANES - HEAD, 2 * LANES), BF16)
    for tile in range(TILES):
        first, end = tile_heads(tile)
        heads = [h for h in (first, first + 1) if h < HEADS]
        state = tile_state(tile)
        parts = []
        for position, head in enumerate(heads):
            inside = (lane < end) if position == 0 else (lane >= end)
            ksum = jnp.broadcast_to(last[:, last_end + head : last_end + head + 1], (HEAD, LANES))
            parts.append(
                jnp.concatenate([jnp.where(inside, state, zero), jnp.where(inside, ksum, zero)], axis=1)
            )
            parts.append(fill)
        weights = jnp.concatenate(parts, axis=0)
        q = q_ref[:, LANES * first : LANES * (first + len(heads))]
        both = jnp.dot(q, weights, preferred_element_type=F32)
        attn = both[:, :LANES] / (both[:, LANES:] + EPS)
        if tile == TILES - 1:
            keep = lax.broadcasted_iota(jnp.int32, attn.shape, 1) < end
            attn = jnp.where(keep, attn, 0.0)
        square = square + attn * attn
        low, high = lane_range(tile)
        attn_ref[:, low:high] = attn[:, : high - low] * rows_ref[9:10, low:high]
    mean = jnp.sum(square, axis=1, keepdims=True) * (1.0 / WIDTH)
    scale_ref[...] = jnp.broadcast_to(lax.rsqrt(mean + 1e-06), scale_ref.shape)

    for tile in range(TILES):
        low, high = lane_range(tile)
        col = lax.broadcasted_iota(jnp.int32, (8, high - low), 0)
        for tap in range(9):
            weight = jnp.broadcast_to(rows_ref[tap : tap + 1, low:high], (8, high - low))
            if tap % 3 == 0:
                weight = jnp.where(col == 7, 0.0, weight)
            if tap % 3 == 2:
                weight = jnp.where(col == 0, 0.0, weight)
            taps[tap, :, low:high] = weight

    rows = tokens // CHUNKS
    frames = rows // 16

    def one_chunk(chunk, carry):
        own = pl.ds(pl.multiple_of(chunk * rows, rows), rows)
        before = pl.ds(pl.multiple_of(tokens + chunk * (rows // 2), rows // 2), rows // 2)
        after = pl.ds(pl.multiple_of(tokens + tokens // 2 + chunk * (rows // 2), rows // 2), rows // 2)
        for tile in range(TILES):
            low, high = lane_range(tile)
            wide = high - low

            def normed(part):
                value = attn_ref[part, low:high] * scale_ref[part, :wide]
                return value.astype(BF16).astype(F32).reshape(-1, 8, wide)

            own_rows = normed(own).reshape(frames, 2, 8, wide)
            four = (normed(before), own_rows[:, 0], own_rows[:, 1], normed(after))
            totals = []
            for out_row in range(2):
                sums = []
                for col_off in range(3):
                    terms = [
                        four[out_row + row_off] * taps[3 * row_off + col_off, :, low:high][None]
                        for row_off in range(3)
                    ]
                    sums.append(terms[0] + terms[1] + terms[2])
                totals.append(pltpu.roll(sums[0], 1, 1) + sums[1] + pltpu.roll(sums[2], 7, 1))
            both = jnp.concatenate([totals[0][:, None], totals[1][:, None]], axis=1)
            out_buf[own, low:high] = both.reshape(rows, wide).astype(BF16)
        pltpu.make_async_copy(out_buf.at[own], out_ref.at[own], sems.at[chunk]).start()
        return carry

    lax.fori_loop(0, CHUNKS, one_chunk, 0)
    for chunk in range(CHUNKS):
        part = slice(rows * chunk, rows * (chunk + 1))
        pltpu.make_async_copy(out_buf.at[part], out_ref.at[part], sems.at[chunk]).wait()


def call(kernel, outs, in_specs, out_specs, scratch=(), flops=1_000_000_000, vmem=VMEM_LIMIT):
    return pl.pallas_call(
        kernel,
        out_shape=outs,
        in_specs=in_specs,
        out_specs=out_specs,
        scratch_shapes=scratch,
        compiler_params=pltpu.CompilerParams(vmem_limit_bytes=vmem),
        cost_estimate=pl.CostEstimate(flops=flops, bytes_accessed=5_000_000, transcendentals=0),
    )


VM = pl.BlockSpec(memory_space=pltpu.VMEM)
SM = pl.BlockSpec(memory_space=pltpu.SMEM)
HB = pl.BlockSpec(memory_space=pltpu.HBM)


def shards(queries, keys, values, gain, conv_weight):
    frames, rows, cols, width = queries.shape
    tokens = frames * rows * cols
    shape = jax.ShapeDtypeStruct
    core = lax.axis_index("core").reshape(1).astype(jnp.int32)

    mine, other = call(
        state_kernel,
        [shape((HALF_ROWS, LANES), F32), shape((HALF_ROWS, LANES), BF16)],
        [SM, HB, HB],
        [VM, VM],
        [
            pltpu.VMEM((tokens, width), BF16),
            pltpu.VMEM((tokens, width), BF16),
            pltpu.VMEM((width, tokens), BF16),
            pltpu.VMEM((2, HEAD * HALF_TILES, LANES), F32),
            pltpu.SemaphoreType.DMA((2, CHUNKS)),
        ],
        vmem=STATE_VMEM,
    )(core, keys.reshape(tokens, width), values.reshape(tokens, width))

    xs, ys, zs = lax.axis_size("x"), lax.axis_size("y"), lax.axis_size("z")
    chunk = HALF_ROWS // (xs * ys)
    both = lax.all_gather(other, "core")
    half = (mine + jnp.where(core == 0, both[1], both[0]).astype(F32)).astype(BF16)
    pieces = lax.all_to_all(half.reshape(xs * ys, chunk, LANES), ("x", "y"), 0, 0, tiled=True)
    totals = call(totals_kernel, shape((zs, xs * chunk, LANES), BF16), [VM], VM)(pieces)

    totals, q_late = lax.optimization_barrier((totals, queries.reshape(tokens, width)))
    border = shape((tokens // 2, TILES * LANES), BF16)
    top, low = call(border_kernel, [border] * 2, [VM], [VM] * 2, flops=20_000_000_000)(q_late)
    size = ys * 2
    up = [(i, i + 1) for i in range(size - 1)]
    down = [(i + 1, i) for i in range(size - 1)]
    q_before = lax.ppermute(low, ("y", "core"), up)
    q_after = lax.ppermute(top, ("y", "core"), down)

    blocks = lax.all_to_all(totals, "z", 0, 0, tiled=True)
    place = lax.axis_index("z").reshape(1).astype(jnp.int32)
    prefix = call(prefix_kernel, shape((xs * ys, chunk, LANES), BF16), [SM, VM], VM, flops=PREFIX_FLOPS)(place, blocks)
    held = lax.all_to_all(prefix, ("x", "y"), 0, 0, tiled=True)
    by_head, taps = call(
        heads_kernel,
        [shape((2 * tokens, HEADS * LANES), BF16), shape((16, TILES * LANES), F32)],
        [VM] * 5,
        [VM] * 2,
    )(q_late, q_before, q_after, gain.reshape(1, width), conv_weight)
    held, by_head, taps = lax.optimization_barrier((held.reshape(HALF_ROWS, LANES), by_head, taps))
    state = lax.all_gather(held, "core")

    padded = TILES * LANES
    out = call(
        readout_kernel,
        shape((tokens, width), BF16),
        [VM] * 3,
        HB,
        [
            pltpu.VMEM((2 * tokens, padded), F32),
            pltpu.VMEM((2 * tokens, LANES), F32),
            pltpu.VMEM((9, 8, padded), F32),
            pltpu.VMEM((tokens, width), BF16),
            pltpu.SemaphoreType.DMA((CHUNKS,)),
        ],
    )(by_head, state, taps)
    return out.reshape(frames, rows, cols, width)


def solution(mesh):
    fine = Mesh(mesh.devices.reshape(4, 8, 8, 2), ("x", "z", "y", "core"))
    tokens = P(("x", "z"), ("y", "core"), None, None)
    return jax.shard_map(
        shards, mesh=fine, in_specs=(tokens, tokens, tokens, P(), P()), out_specs=tokens, check_vma=False
    )
```

```python
import jax
import jax.numpy as jnp
from jax import lax
from jax.experimental import pallas as pl
from jax.experimental.pallas import tpu as pltpu
from jax.sharding import Mesh, PartitionSpec as P

HEAD = 112
WIDTH = 2240
HEADS = WIDTH // HEAD
LANES = 128
TILES = 18
HALF_TILES = TILES // 2
PREFIX_FLOPS = 100_000_000
STATE_VMEM = 55_200_000
CHUNKS = 4
HALF_ROWS = 1024
EPS = 1e-06
F32, BF16 = jnp.float32, jnp.bfloat16
VMEM_LIMIT = 48 * 1024 * 1024


def tile_heads(tile):
    first = tile + tile // 7
    return first, HEAD * (first + 1) - LANES * tile


def lane_range(tile):
    return LANES * tile, min(LANES * (tile + 1), WIDTH)


def state_kernel(core_ref, k_ref, v_ref, mine_ref, other_ref, k_buf, v_buf, kt_ref, state_ref, sems):
    core = core_ref[0]
    tokens = k_buf.shape[0]
    rows = tokens // CHUNKS
    copies = []
    for which, (ref, buf) in enumerate(((k_ref, k_buf), (v_ref, v_buf))):
        for chunk in range(CHUNKS):
            part = slice(rows * chunk, rows * (chunk + 1))
            copies.append(pltpu.make_async_copy(ref.at[part], buf.at[part], sems.at[which, chunk]))
    for copy in copies:
        copy.start()
    for copy in copies[:CHUNKS]:
        copy.wait()
    for tile in range(TILES):
        low, high = lane_range(tile)
        kt_ref[low:high, :] = jnp.maximum(k_buf[:, low:high], 0).T
    lane = lax.broadcasted_iota(jnp.int32, (HEAD, LANES), 1)
    ones = jnp.ones((tokens, LANES), BF16)
    last_end = tile_heads(TILES - 1)[1]
    sums = jnp.zeros((HEAD, LANES), F32)
    for head in range(HEADS):
        ksum = jnp.dot(kt_ref[HEAD * head : HEAD * (head + 1), :], ones, preferred_element_type=F32)
        sums = jnp.where(lane == last_end + head, ksum, sums)
    for copy in copies[CHUNKS:]:
        copy.wait()
    for tile in range(TILES):
        first, end = tile_heads(tile)
        low, high = lane_range(tile)
        v = v_buf[:, low:high]
        if tile < TILES - 1:
            pair = jnp.dot(kt_ref[HEAD * first : HEAD * (first + 2), :], v, preferred_element_type=F32)
            state = jnp.where(lane < end, pair[:HEAD], pair[HEAD:])
        else:
            v = jnp.concatenate([v, jnp.zeros((tokens, LANES - v.shape[1]), BF16)], axis=1)
            state = jnp.dot(kt_ref[HEAD * first : WIDTH, :], v, preferred_element_type=F32)
            state = jnp.where(lane < end, state, sums)
        half, place = divmod(tile, HALF_TILES)
        state_ref[half, HEAD * place : HEAD * (place + 1), :] = state
    rest = HEAD * HALF_TILES
    mine_ref[:rest, :] = state_ref[core]
    other_ref[:rest, :] = state_ref[1 - core].astype(BF16)
    mine_ref[rest:, :] = jnp.zeros((HALF_ROWS - rest, LANES), F32)
    other_ref[rest:, :] = jnp.zeros((HALF_ROWS - rest, LANES), BF16)


def totals_kernel(pieces_ref, out_ref):
    zs = out_ref.shape[0]
    pieces, chunk = pieces_ref.shape[:2]
    xs = out_ref.shape[1] // chunk
    ys = pieces // xs
    for x in range(xs):
        total = pieces_ref[ys * x].astype(F32)
        for y in range(1, ys):
            total = total + pieces_ref[ys * x + y].astype(F32)
        total = total.astype(BF16)
        for z in range(zs):
            out_ref[z, chunk * x : chunk * (x + 1), :] = total


def prefix_kernel(place_ref, blocks_ref, out_ref):
    zs = blocks_ref.shape[0]
    pieces, chunk = out_ref.shape[:2]
    xs = blocks_ref.shape[1] // chunk
    ys = pieces // xs
    place = place_ref[0]
    before = jnp.zeros((chunk, LANES), F32)
    for x in range(xs):
        upto, whole = before, before
        for z in range(zs):
            block = blocks_ref[z, chunk * x : chunk * (x + 1), :].astype(F32)
            upto = upto + jnp.where(z <= place, block, 0.0)
            whole = whole + block
        state = upto.astype(BF16)
        for y in range(ys):
            out_ref[ys * x + y] = state
        before = whole


def border_kernel(q_ref, top_ref, low_ref):
    tokens = q_ref.shape[0]
    for tile in range(TILES):
        low, high = lane_range(tile)
        wide = high - low
        q = jnp.maximum(q_ref[:, low:high], 0).astype(F32).reshape(tokens // 16, 2, 8, wide)
        top_ref[:, low:high] = q[:, 0].reshape(tokens // 2, wide).astype(BF16)
        low_ref[:, low:high] = q[:, 1].reshape(tokens // 2, wide).astype(BF16)
    rest = (tokens // 2, TILES * LANES - WIDTH)
    top_ref[:, WIDTH:] = jnp.zeros(rest, BF16)
    low_ref[:, WIDTH:] = jnp.zeros(rest, BF16)


def heads_kernel(q_ref, before_ref, after_ref, gain_ref, weight_ref, out_ref, rows_ref):
    taps = weight_ref.shape[0]
    rows_ref[:taps, :WIDTH] = weight_ref[...]
    rows_ref[taps : taps + 1, :WIDTH] = gain_ref[...]
    place = 0
    for ref in (q_ref, before_ref, after_ref):
        rows = ref.shape[0]
        fill = jnp.zeros((rows, LANES - HEAD), BF16)
        for head in range(HEADS):
            q = jnp.maximum(ref[:, HEAD * head : HEAD * (head + 1)], 0)
            out_ref[place : place + rows, LANES * head : LANES * (head + 1)] = jnp.concatenate([q, fill], axis=1)
        place += rows


def readout_kernel(
    q_ref, state_ref, rows_ref, out_ref, attn_ref, scale_ref, taps, out_buf, sems
):
    tokens = q_ref.shape[0] // 2
    lane = lax.broadcasted_iota(jnp.int32, (HEAD, LANES), 1)
    zero = jnp.zeros((HEAD, LANES), BF16)

    def tile_state(tile):
        half, place = divmod(tile, HALF_TILES)
        return state_ref[half, HEAD * place : HEAD * (place + 1), :]

    last = tile_state(TILES - 1)
    last_end = tile_heads(TILES - 1)[1]
    square = jnp.zeros((2 * tokens, LANES), F32)
    fill = jnp.zeros((LANES - HEAD, 2 * LANES), BF16)
    for tile in range(TILES):
        first, end = tile_heads(tile)
        heads = [h for h in (first, first + 1) if h < HEADS]
        state = tile_state(tile)
        parts = []
        for position, head in enumerate(heads):
            inside = (lane < end) if position == 0 else (lane >= end)
            ksum = jnp.broadcast_to(last[:, last_end + head : last_end + head + 1], (HEAD, LANES))
            parts.append(
                jnp.concatenate([jnp.where(inside, state, zero), jnp.where(inside, ksum, zero)], axis=1)
            )
            parts.append(fill)
        weights = jnp.concatenate(parts, axis=0)
        q = q_ref[:, LANES * first : LANES * (first + len(heads))]
        both = jnp.dot(q, weights, preferred_element_type=F32)
        attn = both[:, :LANES] / (both[:, LANES:] + EPS)
        if tile == TILES - 1:
            keep = lax.broadcasted_iota(jnp.int32, attn.shape, 1) < end
            attn = jnp.where(keep, attn, 0.0)
        square = square + attn * attn
        low, high = lane_range(tile)
        attn_ref[:, low:high] = attn[:, : high - low] * rows_ref[9:10, low:high]
    mean = jnp.sum(square, axis=1, keepdims=True) * (1.0 / WIDTH)
    scale_ref[...] = jnp.broadcast_to(lax.rsqrt(mean + 1e-06), scale_ref.shape)

    for tile in range(TILES):
        low, high = lane_range(tile)
        col = lax.broadcasted_iota(jnp.int32, (8, high - low), 0)
        for tap in range(9):
            weight = jnp.broadcast_to(rows_ref[tap : tap + 1, low:high], (8, high - low))
            if tap % 3 == 0:
                weight = jnp.where(col == 7, 0.0, weight)
            if tap % 3 == 2:
                weight = jnp.where(col == 0, 0.0, weight)
            taps[tap, :, low:high] = weight

    rows = tokens // CHUNKS
    frames = rows // 16

    def one_chunk(chunk, carry):
        own = pl.ds(pl.multiple_of(chunk * rows, rows), rows)
        before = pl.ds(pl.multiple_of(tokens + chunk * (rows // 2), rows // 2), rows // 2)
        after = pl.ds(pl.multiple_of(tokens + tokens // 2 + chunk * (rows // 2), rows // 2), rows // 2)
        for tile in range(TILES):
            low, high = lane_range(tile)
            wide = high - low

            def normed(part):
                value = attn_ref[part, low:high] * scale_ref[part, :wide]
                return value.astype(BF16).astype(F32).reshape(-1, 8, wide)

            own_rows = normed(own).reshape(frames, 2, 8, wide)
            four = (normed(before), own_rows[:, 0], own_rows[:, 1], normed(after))
            totals = []
            for out_row in range(2):
                sums = []
                for col_off in range(3):
                    terms = [
                        four[out_row + row_off] * taps[3 * row_off + col_off, :, low:high][None]
                        for row_off in range(3)
                    ]
                    sums.append(terms[0] + terms[1] + terms[2])
                totals.append(pltpu.roll(sums[0], 1, 1) + sums[1] + pltpu.roll(sums[2], 7, 1))
            both = jnp.concatenate([totals[0][:, None], totals[1][:, None]], axis=1)
            out_buf[own, low:high] = both.reshape(rows, wide).astype(BF16)
        pltpu.make_async_copy(out_buf.at[own], out_ref.at[own], sems.at[chunk]).start()
        return carry

    lax.fori_loop(0, CHUNKS, one_chunk, 0)
    for chunk in range(CHUNKS):
        part = slice(rows * chunk, rows * (chunk + 1))
        pltpu.make_async_copy(out_buf.at[part], out_ref.at[part], sems.at[chunk]).wait()


def call(kernel, outs, in_specs, out_specs, scratch=(), flops=1_000_000_000, vmem=VMEM_LIMIT):
    return pl.pallas_call(
        kernel,
        out_shape=outs,
        in_specs=in_specs,
        out_specs=out_specs,
        scratch_shapes=scratch,
        compiler_params=pltpu.CompilerParams(vmem_limit_bytes=vmem),
        cost_estimate=pl.CostEstimate(flops=flops, bytes_accessed=5_000_000, transcendentals=0),
    )


VM = pl.BlockSpec(memory_space=pltpu.VMEM)
SM = pl.BlockSpec(memory_space=pltpu.SMEM)
HB = pl.BlockSpec(memory_space=pltpu.HBM)


def shards(queries, keys, values, gain, conv_weight):
    frames, rows, cols, width = queries.shape
    tokens = frames * rows * cols
    shape = jax.ShapeDtypeStruct
    core = lax.axis_index("core").reshape(1).astype(jnp.int32)

    mine, other = call(
        state_kernel,
        [shape((HALF_ROWS, LANES), F32), shape((HALF_ROWS, LANES), BF16)],
        [SM, HB, HB],
        [VM, VM],
        [
            pltpu.VMEM((tokens, width), BF16),
            pltpu.VMEM((tokens, width), BF16),
            pltpu.VMEM((width, tokens), BF16),
            pltpu.VMEM((2, HEAD * HALF_TILES, LANES), F32),
            pltpu.SemaphoreType.DMA((2, CHUNKS)),
        ],
        vmem=STATE_VMEM,
    )(core, keys.reshape(tokens, width), values.reshape(tokens, width))

    xs, ys, zs = lax.axis_size("x"), lax.axis_size("y"), lax.axis_size("z")
    chunk = HALF_ROWS // (xs * ys)
    both = lax.all_gather(other, "core")
    half = (mine + jnp.where(core == 0, both[1], both[0]).astype(F32)).astype(BF16)
    half, q_late = lax.optimization_barrier((half, queries.reshape(tokens, width)))
    border = shape((tokens // 2, TILES * LANES), BF16)
    top, low = call(border_kernel, [border] * 2, [VM], [VM] * 2, flops=20_000_000_000)(q_late)
    size = ys * 2
    up = [(i, i + 1) for i in range(size - 1)]
    down = [(i + 1, i) for i in range(size - 1)]
    q_before = lax.ppermute(low, ("y", "core"), up)
    q_after = lax.ppermute(top, ("y", "core"), down)

    pieces = lax.all_to_all(half.reshape(xs * ys, chunk, LANES), ("x", "y"), 0, 0, tiled=True)
    totals = call(totals_kernel, shape((zs, xs * chunk, LANES), BF16), [VM], VM)(pieces)

    blocks = lax.all_to_all(totals, "z", 0, 0, tiled=True)
    by_head, taps = call(
        heads_kernel,
        [shape((2 * tokens, HEADS * LANES), BF16), shape((16, TILES * LANES), F32)],
        [VM] * 5,
        [VM] * 2,
    )(q_late, q_before, q_after, gain.reshape(1, width), conv_weight)
    blocks, by_head, taps = lax.optimization_barrier((blocks, by_head, taps))
    place = lax.axis_index("z").reshape(1).astype(jnp.int32)
    prefix = call(prefix_kernel, shape((xs * ys, chunk, LANES), BF16), [SM, VM], VM, flops=PREFIX_FLOPS)(place, blocks)
    held = lax.all_to_all(prefix, ("x", "y"), 0, 0, tiled=True)
    held = held.reshape(HALF_ROWS, LANES)
    state = lax.all_gather(held, "core")

    padded = TILES * LANES
    out = call(
        readout_kernel,
        shape((tokens, width), BF16),
        [VM] * 3,
        HB,
        [
            pltpu.VMEM((2 * tokens, padded), F32),
            pltpu.VMEM((2 * tokens, LANES), F32),
            pltpu.VMEM((9, 8, padded), F32),
            pltpu.VMEM((tokens, width), BF16),
            pltpu.SemaphoreType.DMA((CHUNKS,)),
        ],
    )(by_head, state, taps)
    return out.reshape(frames, rows, cols, width)


def solution(mesh):
    fine = Mesh(mesh.devices.reshape(4, 8, 8, 2), ("x", "z", "y", "core"))
    tokens = P(("x", "z"), ("y", "core"), None, None)
    return jax.shard_map(
        shards, mesh=fine, in_specs=(tokens, tokens, tokens, P(), P()), out_specs=tokens, check_vma=False
    )
```

```python
import jax
import jax.numpy as jnp
from jax import lax
from jax.experimental import pallas as pl
from jax.experimental.pallas import tpu as pltpu
from jax.sharding import Mesh, PartitionSpec as P

HEAD = 112
WIDTH = 2240
HEADS = WIDTH // HEAD
LANES = 128
TILES = 18
HALF_TILES = TILES // 2
PREFIX_FLOPS = 100_000_000
STATE_VMEM = 55_200_000
LOADS = 2
CHUNKS = 4
HALF_ROWS = 1024
EPS = 1e-06
F32, BF16 = jnp.float32, jnp.bfloat16
VMEM_LIMIT = 48 * 1024 * 1024


def tile_heads(tile):
    first = tile + tile // 7
    return first, HEAD * (first + 1) - LANES * tile


def lane_range(tile):
    return LANES * tile, min(LANES * (tile + 1), WIDTH)


def state_kernel(core_ref, k_ref, v_ref, mine_ref, other_ref, k_buf, v_buf, kt_ref, state_ref, sems):
    core = core_ref[0]
    tokens = k_buf.shape[0]
    rows = tokens // LOADS
    copies = []
    for which, (ref, buf) in enumerate(((k_ref, k_buf), (v_ref, v_buf))):
        for chunk in range(LOADS):
            part = slice(rows * chunk, rows * (chunk + 1))
            copies.append(pltpu.make_async_copy(ref.at[part], buf.at[part], sems.at[which, chunk]))
    for copy in copies:
        copy.start()
    for copy in copies[:LOADS]:
        copy.wait()
    for tile in range(TILES):
        low, high = lane_range(tile)
        kt_ref[low:high, :] = jnp.maximum(k_buf[:, low:high], 0).T
    lane = lax.broadcasted_iota(jnp.int32, (HEAD, LANES), 1)
    ones = jnp.ones((tokens, LANES), BF16)
    last_end = tile_heads(TILES - 1)[1]
    sums = jnp.zeros((HEAD, LANES), F32)
    for head in range(HEADS):
        ksum = jnp.dot(kt_ref[HEAD * head : HEAD * (head + 1), :], ones, preferred_element_type=F32)
        sums = jnp.where(lane == last_end + head, ksum, sums)
    for copy in copies[LOADS:]:
        copy.wait()
    for tile in range(TILES):
        first, end = tile_heads(tile)
        low, high = lane_range(tile)
        v = v_buf[:, low:high]
        if tile < TILES - 1:
            pair = jnp.dot(kt_ref[HEAD * first : HEAD * (first + 2), :], v, preferred_element_type=F32)
            state = jnp.where(lane < end, pair[:HEAD], pair[HEAD:])
        else:
            v = jnp.concatenate([v, jnp.zeros((tokens, LANES - v.shape[1]), BF16)], axis=1)
            state = jnp.dot(kt_ref[HEAD * first : WIDTH, :], v, preferred_element_type=F32)
            state = jnp.where(lane < end, state, sums)
        half, place = divmod(tile, HALF_TILES)
        state_ref[half, HEAD * place : HEAD * (place + 1), :] = state
    rest = HEAD * HALF_TILES
    mine_ref[:rest, :] = state_ref[core]
    other_ref[:rest, :] = state_ref[1 - core].astype(BF16)
    mine_ref[rest:, :] = jnp.zeros((HALF_ROWS - rest, LANES), F32)
    other_ref[rest:, :] = jnp.zeros((HALF_ROWS - rest, LANES), BF16)


def totals_kernel(pieces_ref, out_ref):
    zs = out_ref.shape[0]
    pieces, chunk = pieces_ref.shape[:2]
    xs = out_ref.shape[1] // chunk
    ys = pieces // xs
    for x in range(xs):
        total = pieces_ref[ys * x].astype(F32)
        for y in range(1, ys):
            total = total + pieces_ref[ys * x + y].astype(F32)
        total = total.astype(BF16)
        for z in range(zs):
            out_ref[z, chunk * x : chunk * (x + 1), :] = total


def prefix_kernel(place_ref, blocks_ref, out_ref):
    zs = blocks_ref.shape[0]
    pieces, chunk = out_ref.shape[:2]
    xs = blocks_ref.shape[1] // chunk
    ys = pieces // xs
    place = place_ref[0]
    before = jnp.zeros((chunk, LANES), F32)
    for x in range(xs):
        upto, whole = before, before
        for z in range(zs):
            block = blocks_ref[z, chunk * x : chunk * (x + 1), :].astype(F32)
            upto = upto + jnp.where(z <= place, block, 0.0)
            whole = whole + block
        state = upto.astype(BF16)
        for y in range(ys):
            out_ref[ys * x + y] = state
        before = whole


def border_kernel(q_ref, top_ref, low_ref):
    tokens = q_ref.shape[0]
    for tile in range(TILES):
        low, high = lane_range(tile)
        wide = high - low
        q = jnp.maximum(q_ref[:, low:high], 0).astype(F32).reshape(tokens // 16, 2, 8, wide)
        top_ref[:, low:high] = q[:, 0].reshape(tokens // 2, wide).astype(BF16)
        low_ref[:, low:high] = q[:, 1].reshape(tokens // 2, wide).astype(BF16)
    rest = (tokens // 2, TILES * LANES - WIDTH)
    top_ref[:, WIDTH:] = jnp.zeros(rest, BF16)
    low_ref[:, WIDTH:] = jnp.zeros(rest, BF16)


def heads_kernel(q_ref, before_ref, after_ref, gain_ref, weight_ref, out_ref, rows_ref):
    taps = weight_ref.shape[0]
    rows_ref[:taps, :WIDTH] = weight_ref[...]
    rows_ref[taps : taps + 1, :WIDTH] = gain_ref[...]
    place = 0
    for ref in (q_ref, before_ref, after_ref):
        rows = ref.shape[0]
        fill = jnp.zeros((rows, LANES - HEAD), BF16)
        for head in range(HEADS):
            q = jnp.maximum(ref[:, HEAD * head : HEAD * (head + 1)], 0)
            out_ref[place : place + rows, LANES * head : LANES * (head + 1)] = jnp.concatenate([q, fill], axis=1)
        place += rows


def readout_kernel(
    q_ref, state_ref, rows_ref, out_ref, attn_ref, scale_ref, taps, out_buf, sems
):
    tokens = q_ref.shape[0] // 2
    lane = lax.broadcasted_iota(jnp.int32, (HEAD, LANES), 1)
    zero = jnp.zeros((HEAD, LANES), BF16)

    def tile_state(tile):
        half, place = divmod(tile, HALF_TILES)
        return state_ref[half, HEAD * place : HEAD * (place + 1), :]

    last = tile_state(TILES - 1)
    last_end = tile_heads(TILES - 1)[1]
    square = jnp.zeros((2 * tokens, LANES), F32)
    fill = jnp.zeros((LANES - HEAD, 2 * LANES), BF16)
    for tile in range(TILES):
        first, end = tile_heads(tile)
        heads = [h for h in (first, first + 1) if h < HEADS]
        state = tile_state(tile)
        parts = []
        for position, head in enumerate(heads):
            inside = (lane < end) if position == 0 else (lane >= end)
            ksum = jnp.broadcast_to(last[:, last_end + head : last_end + head + 1], (HEAD, LANES))
            parts.append(
                jnp.concatenate([jnp.where(inside, state, zero), jnp.where(inside, ksum, zero)], axis=1)
            )
            parts.append(fill)
        weights = jnp.concatenate(parts, axis=0)
        q = q_ref[:, LANES * first : LANES * (first + len(heads))]
        both = jnp.dot(q, weights, preferred_element_type=F32)
        attn = both[:, :LANES] / (both[:, LANES:] + EPS)
        square = square + attn * attn
        low, high = lane_range(tile)
        attn_ref[:, low:high] = attn[:, : high - low] * rows_ref[9:10, low:high]
    mean = jnp.sum(square, axis=1, keepdims=True) * (1.0 / WIDTH)
    scale_ref[...] = jnp.broadcast_to(lax.rsqrt(mean + 1e-06), scale_ref.shape)

    for tile in range(TILES):
        low, high = lane_range(tile)
        col = lax.broadcasted_iota(jnp.int32, (8, high - low), 0)
        for tap in range(9):
            weight = jnp.broadcast_to(rows_ref[tap : tap + 1, low:high], (8, high - low))
            if tap % 3 == 0:
                weight = jnp.where(col == 7, 0.0, weight)
            if tap % 3 == 2:
                weight = jnp.where(col == 0, 0.0, weight)
            taps[tap, :, low:high] = weight

    rows = tokens // CHUNKS
    frames = rows // 16

    def one_chunk(chunk, carry):
        own = pl.ds(pl.multiple_of(chunk * rows, rows), rows)
        before = pl.ds(pl.multiple_of(tokens + chunk * (rows // 2), rows // 2), rows // 2)
        after = pl.ds(pl.multiple_of(tokens + tokens // 2 + chunk * (rows // 2), rows // 2), rows // 2)
        for tile in range(TILES):
            low, high = lane_range(tile)
            wide = high - low

            def normed(part):
                value = attn_ref[part, low:high] * scale_ref[part, :wide]
                return value.astype(BF16).astype(F32).reshape(-1, 8, wide)

            own_rows = normed(own).reshape(frames, 2, 8, wide)
            four = (normed(before), own_rows[:, 0], own_rows[:, 1], normed(after))
            totals = []
            for out_row in range(2):
                sums = []
                for col_off in range(3):
                    terms = [
                        four[out_row + row_off] * taps[3 * row_off + col_off, :, low:high][None]
                        for row_off in range(3)
                    ]
                    sums.append(terms[0] + terms[1] + terms[2])
                totals.append(pltpu.roll(sums[0], 1, 1) + sums[1] + pltpu.roll(sums[2], 7, 1))
            both = jnp.concatenate([totals[0][:, None], totals[1][:, None]], axis=1)
            out_buf[own, low:high] = both.reshape(rows, wide).astype(BF16)
        pltpu.make_async_copy(out_buf.at[own], out_ref.at[own], sems.at[chunk]).start()
        return carry

    lax.fori_loop(0, CHUNKS, one_chunk, 0)
    for chunk in range(CHUNKS):
        part = slice(rows * chunk, rows * (chunk + 1))
        pltpu.make_async_copy(out_buf.at[part], out_ref.at[part], sems.at[chunk]).wait()


def call(kernel, outs, in_specs, out_specs, scratch=(), flops=1_000_000_000, vmem=VMEM_LIMIT):
    return pl.pallas_call(
        kernel,
        out_shape=outs,
        in_specs=in_specs,
        out_specs=out_specs,
        scratch_shapes=scratch,
        compiler_params=pltpu.CompilerParams(vmem_limit_bytes=vmem),
        cost_estimate=pl.CostEstimate(flops=flops, bytes_accessed=5_000_000, transcendentals=0),
    )


VM = pl.BlockSpec(memory_space=pltpu.VMEM)
SM = pl.BlockSpec(memory_space=pltpu.SMEM)
HB = pl.BlockSpec(memory_space=pltpu.HBM)


def shards(queries, keys, values, gain, conv_weight):
    frames, rows, cols, width = queries.shape
    tokens = frames * rows * cols
    shape = jax.ShapeDtypeStruct
    core = lax.axis_index("core").reshape(1).astype(jnp.int32)

    mine, other = call(
        state_kernel,
        [shape((HALF_ROWS, LANES), F32), shape((HALF_ROWS, LANES), BF16)],
        [SM, HB, HB],
        [VM, VM],
        [
            pltpu.VMEM((tokens, width), BF16),
            pltpu.VMEM((tokens, width), BF16),
            pltpu.VMEM((width, tokens), BF16),
            pltpu.VMEM((2, HEAD * HALF_TILES, LANES), F32),
            pltpu.SemaphoreType.DMA((2, LOADS)),
        ],
        vmem=STATE_VMEM,
    )(core, keys.reshape(tokens, width), values.reshape(tokens, width))

    xs, ys, zs = lax.axis_size("x"), lax.axis_size("y"), lax.axis_size("z")
    chunk = HALF_ROWS // (xs * ys)
    both = lax.all_gather(other, "core")
    half = (mine + jnp.where(core == 0, both[1], both[0]).astype(F32)).astype(BF16)
    half, q_late = lax.optimization_barrier((half, queries.reshape(tokens, width)))
    border = shape((tokens // 2, TILES * LANES), BF16)
    top, low = call(border_kernel, [border] * 2, [VM], [VM] * 2, flops=20_000_000_000)(q_late)
    size = ys * 2
    up = [(i, i + 1) for i in range(size - 1)]
    down = [(i + 1, i) for i in range(size - 1)]
    q_before = lax.ppermute(low, ("y", "core"), up)
    q_after = lax.ppermute(top, ("y", "core"), down)

    pieces = lax.all_to_all(half.reshape(xs * ys, chunk, LANES), ("x", "y"), 0, 0, tiled=True)
    totals = call(totals_kernel, shape((zs, xs * chunk, LANES), BF16), [VM], VM)(pieces)

    blocks = lax.all_to_all(totals, "z", 0, 0, tiled=True)
    by_head, taps = call(
        heads_kernel,
        [shape((2 * tokens, HEADS * LANES), BF16), shape((16, TILES * LANES), F32)],
        [VM] * 5,
        [VM] * 2,
    )(q_late, q_before, q_after, gain.reshape(1, width), conv_weight)
    blocks, by_head, taps = lax.optimization_barrier((blocks, by_head, taps))
    place = lax.axis_index("z").reshape(1).astype(jnp.int32)
    prefix = call(prefix_kernel, shape((xs * ys, chunk, LANES), BF16), [SM, VM], VM, flops=PREFIX_FLOPS)(place, blocks)
    held = lax.all_to_all(prefix, ("x", "y"), 0, 0, tiled=True)
    held = held.reshape(HALF_ROWS, LANES)
    state = lax.all_gather(held, "core")

    padded = TILES * LANES
    out = call(
        readout_kernel,
        shape((tokens, width), BF16),
        [VM] * 3,
        HB,
        [
            pltpu.VMEM((2 * tokens, padded), F32),
            pltpu.VMEM((2 * tokens, LANES), F32),
            pltpu.VMEM((9, 8, padded), F32),
            pltpu.VMEM((tokens, width), BF16),
            pltpu.SemaphoreType.DMA((CHUNKS,)),
        ],
    )(by_head, state, taps)
    return out.reshape(frames, rows, cols, width)


def solution(mesh):
    fine = Mesh(mesh.devices.reshape(4, 8, 8, 2), ("x", "z", "y", "core"))
    tokens = P(("x", "z"), ("y", "core"), None, None)
    return jax.shard_map(
        shards, mesh=fine, in_specs=(tokens, tokens, tokens, P(), P()), out_specs=tokens, check_vma=False
    )
```
